512 devices in a mesh: req: 64 (over x, z), kv: 8 (over y, core).
Axes of the slice: x: 4, y: 4, z: 16, core: 2. Of those that a mesh axis runs over, the one named last changes fastest.
Arguments:
- queries: bfloat16 [1024, 8, 8192], P(('req', 'kv')), may hold values from -6 to 6
- new_keys: bfloat16 [1024, 8, 1024], P(('req', 'kv')), may hold values from -6 to 6
- new_values: bfloat16 [1024, 8, 1024], P(('req', 'kv')), may hold values from -6 to 6
- suffix_keys: bfloat16 [1024, 64, 1024], P('req', None, 'kv'), may hold values from -6 to 6
- suffix_values: bfloat16 [1024, 64, 1024], P('req', None, 'kv'), may hold values from -6 to 6
- suffix_len: int32 [1024], P('req'), may hold values from 1 to 64, 32768 in all
- prompt_keys: bfloat16 [128, 128, 1024], P('req', None, 'kv'), may hold values from -6 to 6
- prompt_values: bfloat16 [128, 128, 1024], P('req', None, 'kv'), may hold values from -6 to 6
- parent: int32 [128], P('req'), may hold values from -1 to 0, as said below
- prompt_owner: int32 [1024], P('req'), may hold values from 0 to 63, as said below
- prompt_node: int32 [1024], P('req'), may hold values from 0 to 1
Outputs:
- attended: bfloat16 [1024, 8, 8192], P(('req', 'kv'))
The draws below stay inside these ranges and needn't reach their ends.
Inputs may be any that keep to these rules, and one draw needn't show every extreme that they name: `prompt_owner`: among the 16 requests of one device of req, no owner appears more than 2 times; one owner, the same for every device, appears exactly 2 times on each device. Within each device's 2 blocks the parent of block j is -1 or a block j' < j of the same device; block 0 is always a root.
All inputs are finite; a program needn't handle non-finite values. No bound on the sum of `suffix_len` on one device may be relied on, other than what follows from the above.
Results may differ from the reference program's by a relative error of at most 0.0043.
Values may be sent and summed in bfloat16 or wider, within the bound.
A program may use at most 64 MiB of HBM per device.

```python
import math
import jax
import jax.numpy as jnp
import numpy as np
from jax import lax

QH = 64
KVH = 8
HD = 128
BLK = 128
STEPS = 8
PB = 2
SUF = 64
R_DEV = 16
CAP = 2
ROWS = 1024
NB = 128
N_REQ = 64


def draw_queries(key, part):
    key = jax.random.fold_in(key, 1)
    noise_key = jax.random.fold_in(key, 0)
    base = jax.random.normal(noise_key, (ROWS, STEPS, KVH, QH // KVH, HD), jnp.float32)
    return jnp.clip(base, -6.0, 6.0).reshape(ROWS, STEPS, QH * HD).astype(jnp.bfloat16)


def draw_new_keys(key, part):
    key = jax.random.fold_in(key, 2)
    noise_key = jax.random.fold_in(key, 0)
    base = jax.random.normal(noise_key, (ROWS, STEPS, KVH, HD), jnp.float32)
    return jnp.clip(base, -6.0, 6.0).reshape(ROWS, STEPS, KVH * HD).astype(jnp.bfloat16)


def draw_suffix_keys(key, part):
    key = jax.random.fold_in(key, 3)
    noise_key = jax.random.fold_in(key, 0)
    base = jax.random.normal(noise_key, (ROWS, SUF, KVH, HD), jnp.float32)
    return jnp.clip(base, -6.0, 6.0).reshape(ROWS, SUF, KVH * HD).astype(jnp.bfloat16)


def draw_prompt_keys(key, part):
    key = jax.random.fold_in(key, 6)
    noise_key = jax.random.fold_in(key, 0)
    base = jax.random.normal(noise_key, (NB, BLK, KVH, HD), jnp.float32)
    return jnp.clip(base, -6.0, 6.0).reshape(NB, BLK, KVH * HD).astype(jnp.bfloat16)


def draw_prompt_owner(key, part):
    key = jax.random.fold_in(key, 4)
    hot_key, row_key = jax.random.split(key)
    hot_owner = jax.random.randint(hot_key, (), 0, N_REQ)
    others = (hot_owner + 1 + jnp.arange((N_REQ - 1) * CAP) // CAP) % N_REQ

    def one_device(device_key):
        first_key, second_key = jax.random.split(device_key)
        remaining = jax.random.permutation(first_key, others)[:R_DEV - CAP]
        filled = jnp.concatenate([jnp.full((CAP,), hot_owner, dtype=others.dtype), remaining])
        return jax.random.permutation(second_key, filled)
    device_keys = jax.random.split(row_key, N_REQ)
    return jax.vmap(one_device)(device_keys).reshape(ROWS).astype(jnp.int32)


def draw_parent(key, part):
    key = jax.random.fold_in(key, 5)
    raw_key, device_key = jax.random.split(key)
    raw_bits = jax.random.randint(raw_key, (N_REQ, PB), 0, 1 << 20)
    limits = jnp.arange(PB, dtype=jnp.int32) + 1
    parents = raw_bits % limits[None, :] - 1
    forced_device = jax.random.randint(device_key, (), 0, N_REQ)
    forced = (jnp.arange(N_REQ)[:, None] == forced_device) & (jnp.arange(PB)[None, :] == PB - 1)
    parents = jnp.where(forced, PB - 2, parents)
    return parents.reshape(N_REQ * PB).astype(jnp.int32)


def with_ends(result, stream_key, smallest, largest):
    longest = result.shape.index(max(result.shape))
    spots = []
    for shift in (0, 1):
        where = [jax.random.randint(jax.random.fold_in(stream_key, axis), (), 0, length) for axis, length in enumerate(result.shape)]
        where[longest] = (where[longest] + shift) % result.shape[longest]
        spots.append(tuple(where))
    return result.at[spots[0]].set(smallest).at[spots[1]].set(largest)


def levels(own_key, extent, pieces, smallest, largest):
    level, own = 1.0, jax.random.fold_in(own_key, 6)
    for axis_at, blocks in pieces:
        steps = jnp.exp(jax.random.uniform(jax.random.fold_in(own, axis_at), (blocks,), jnp.float32, smallest / len(pieces), largest / len(pieces)))
        level = level * jnp.repeat(steps, extent[axis_at] // blocks).reshape([-1 if axis == axis_at else 1 for axis in range(len(extent))])
    return level


def profile(number_of, total, most, skew):
    loads = [(1 << 20) // math.isqrt(rank ** skew) + 1 for rank in range(2, number_of + 1)]
    spare, counts = total - most - (number_of - 1), [1] * (number_of - 1)
    while spare > 0:
        movable = [i for i in range(number_of - 1) if counts[i] < most]
        whole, left = sum([loads[i] for i in movable]), spare
        for i in movable:
            more = min(most - counts[i], max(1, left * loads[i] // whole), spare)
            counts[i] = counts[i] + more
            spare = spare - more
    return np.array([most] + counts)


def ragged(stream_key, count, total, limit, skew):
    if count == 2:
        one = jax.random.randint(stream_key, (), max(1, total - limit), min(limit, total - 1) + 1)
        return jnp.stack([one, total - one])
    tallies = jnp.asarray(profile(count, total, limit, skew), jnp.int32)
    pairs = (count - 1) // 2
    donor, taker = tallies[1:1 + 2 * pairs:2], tallies[2:2 + 2 * pairs:2]
    room = jnp.minimum(donor - 1, limit - taker)
    passed = jax.random.randint(jax.random.fold_in(stream_key, 1), (pairs,), 0, 1 << 20) % (room + 1)
    tallies = tallies.at[1:1 + 2 * pairs:2].set(donor - passed).at[2:2 + 2 * pairs:2].set(taker + passed)
    return tallies[jax.random.permutation(jax.random.fold_in(stream_key, 2), count)]


def normal_values(own_key, extent, width, reach, shards=(), held_as=jnp.bfloat16):
    result = jax.random.normal(own_key, extent, jnp.float32) * width
    if len(shards) > 0:
        result = levels(own_key, extent, shards, -0.22, 0.18) * result
    return jnp.clip(result, min=-reach, max=reach).astype(held_as)


def setup_inputs(seed: int = 0) -> dict:
    keys = jax.random.split(jax.random.key(seed), 12)
    return {
        "queries": draw_queries(jax.random.fold_in(keys[11], 71), 0),
        "new_keys": draw_new_keys(jax.random.fold_in(keys[11], 71), 0),
        "new_values": normal_values(keys[2], (ROWS, STEPS, KVH * HD), 1.0, 6.0, ((0, 512),)),
        "suffix_keys": draw_suffix_keys(jax.random.fold_in(keys[11], 71), 0),
        "suffix_values": normal_values(keys[4], (ROWS, SUF, KVH * HD), 1.0, 6.0, ((0, 64), (2, 8))),
        "suffix_len": ragged(keys[5], ROWS, ROWS * SUF // 2, SUF, 2).astype(jnp.int32),
        "prompt_keys": draw_prompt_keys(jax.random.fold_in(keys[11], 71), 0),
        "prompt_values": normal_values(keys[7], (NB, BLK, KVH * HD), 1.0, 6.0, ((0, 64), (2, 8))),
        "parent": draw_parent(jax.random.fold_in(keys[11], 71), 0),
        "prompt_owner": draw_prompt_owner(jax.random.fold_in(keys[11], 71), 0),
        "prompt_node": with_ends(jax.random.randint(keys[10], (ROWS,), 0, PB), jax.random.fold_in(keys[10], 1), 0, PB - 1).astype(jnp.int32),
    }


def ancestry(tree_parent):
    width_nodes = tree_parent.shape[-1]
    node_ids = jnp.arange(width_nodes, dtype=jnp.int32)
    current = jnp.broadcast_to(node_ids, tree_parent.shape).astype(jnp.int32)
    ancestors = jnp.zeros(tree_parent.shape + (width_nodes,), jnp.float32)
    for depth_step in range(width_nodes):
        at_node = current[..., None] == node_ids
        ancestors = jnp.maximum(ancestors, at_node.astype(jnp.float32))
        upward = lax.optimization_barrier(jnp.sum(jnp.where(at_node, tree_parent[..., None, :], 0), axis=-1)).astype(jnp.int32)
        current = jnp.where(current >= 0, upward, -1).astype(jnp.int32)
    return ancestors

def merge_parts(prompt_out, prompt_lse, own_out, own_lse):
    highest = jnp.maximum(prompt_lse, own_lse)
    prompt_weight = jnp.exp(prompt_lse - highest)
    own_weight = jnp.exp(own_lse - highest)
    mixed = prompt_weight[..., None] * prompt_out + own_weight[..., None] * own_out
    return mixed / (prompt_weight + own_weight)[..., None]

def to_bf16_values(weights):
    return lax.optimization_barrier(weights.astype(jnp.bfloat16)).astype(jnp.float32)

def reference(queries, new_keys, new_values, suffix_keys, suffix_values, suffix_len, prompt_keys, prompt_values, parent, prompt_owner, prompt_node):
    group_size = QH // KVH
    scaling = 1.0 / math.sqrt(HD)
    ancestors = ancestry(parent.reshape(N_REQ, PB))
    pool_keys = prompt_keys.reshape(N_REQ, PB, BLK, KVH, HD)
    pool_values = prompt_values.reshape(N_REQ, PB, BLK, KVH, HD)
    suffix_pos = jnp.arange(SUF, dtype=jnp.int32)
    step_pos = jnp.arange(STEPS, dtype=jnp.int32)
    fresh_ok = (step_pos[None, :] <= step_pos[:, None])[None, :, None, None, :]

    def device_rows(block_index):
        row_start = (block_index * R_DEV).astype(jnp.int32)

        def slice_rows(array):
            return lax.dynamic_slice_in_dim(array, row_start, R_DEV, 0)
        query_rows = slice_rows(queries).astype(jnp.float32).reshape(R_DEV, STEPS, KVH, group_size, HD)
        owners = slice_rows(prompt_owner)
        nodes_here = slice_rows(prompt_node)
        block_keys = pool_keys[owners].astype(jnp.float32)
        block_values = pool_values[owners].astype(jnp.float32)
        live_blocks = ancestors[owners, nodes_here] > 0.5
        scores = jnp.einsum('rtgjd,rbwgd->rtgjbw', query_rows, block_keys) * scaling
        usable = live_blocks[:, None, None, None, :, None]
        highest = lax.optimization_barrier(jnp.max(jnp.where(usable, scores, -jnp.inf), axis=(4, 5)))
        weights = jnp.where(usable, jnp.exp(scores - highest[..., None, None]), 0.0)
        weight_sum = lax.optimization_barrier(jnp.sum(weights, axis=(4, 5)))
        numerator = jnp.einsum('rtgjbw,rbwgd->rtgjd', to_bf16_values(weights), block_values)
        prompt_out = numerator / weight_sum[..., None]
        prompt_lse = highest + jnp.log(weight_sum)
        own_keys = slice_rows(suffix_keys).astype(jnp.float32).reshape(R_DEV, SUF, KVH, HD)
        own_values = slice_rows(suffix_values).astype(jnp.float32).reshape(R_DEV, SUF, KVH, HD)
        fresh_keys = slice_rows(new_keys).astype(jnp.float32).reshape(R_DEV, STEPS, KVH, HD)
        fresh_values = slice_rows(new_values).astype(jnp.float32).reshape(R_DEV, STEPS, KVH, HD)
        lengths = slice_rows(suffix_len)
        suffix_scores = jnp.einsum('rtgjd,rkgd->rtgjk', query_rows, own_keys) * scaling
        fresh_scores = jnp.einsum('rtgjd,rkgd->rtgjk', query_rows, fresh_keys) * scaling
        suffix_ok = (suffix_pos[None, :] < lengths[:, None])[:, None, None, None, :]
        own_high = jnp.maximum(lax.optimization_barrier(jnp.max(jnp.where(suffix_ok, suffix_scores, -jnp.inf), axis=-1)), lax.optimization_barrier(jnp.max(jnp.where(fresh_ok, fresh_scores, -jnp.inf), axis=-1)))
        suffix_weights = jnp.where(suffix_ok, jnp.exp(suffix_scores - own_high[..., None]), 0.0)
        fresh_weights = jnp.where(fresh_ok, jnp.exp(fresh_scores - own_high[..., None]), 0.0)
        own_sum = lax.optimization_barrier(jnp.sum(suffix_weights, axis=-1)) + lax.optimization_barrier(jnp.sum(fresh_weights, axis=-1))
        own_numerator = jnp.einsum('rtgjk,rkgd->rtgjd', to_bf16_values(suffix_weights), own_values)
        own_numerator = own_numerator + jnp.einsum('rtgjk,rkgd->rtgjd', to_bf16_values(fresh_weights), fresh_values)
        own_out = own_numerator / own_sum[..., None]
        own_lse = own_high + jnp.log(own_sum)
        mixed = merge_parts(prompt_out, prompt_lse, own_out, own_lse)
        return mixed.astype(jnp.bfloat16).reshape(R_DEV, STEPS, QH * HD)
    blocks = lax.map(device_rows, jnp.arange(N_REQ, dtype=jnp.int32))
    return blocks.reshape(ROWS, STEPS, QH * HD)
```

```python
import functools
import math

import jax
import jax.numpy as jnp
from jax import lax
from jax.experimental import pallas as pl
from jax.experimental.pallas import tpu as pltpu
from jax.sharding import PartitionSpec as P

MESH = pl.DeviceIdType.MESH
BF16, F32, I32 = jnp.bfloat16, jnp.float32, jnp.int32

HD = 128
BLK = 128
STEPS = 8
GROUP = 8
SUF = 64
NX = 4
PIECES = 2
FLAG = 16
LOW = -1e30
EXPO = math.log2(math.e) / math.sqrt(HD)

NN = (((1,), (0,)), ((), ()))
NT = (((1,), (1,)), ((), ()))


def dot(a, b, dims=NN):
    return lax.dot_general(a, b, dims, preferred_element_type=F32)


def ring_tree(half):
    return {d: d - 1 for d in range(1, half + 1)}


LAGS = (2, 4)


def kernel(
    nz, nkv,
    q_hbm, nk_hbm, nv_hbm, sk_hbm, sv_hbm, pk_hbm, pv_hbm, len_hbm, par_hbm, owner_hbm, node_hbm,
    out_ref,
    k_all, v_nat, v_all, q_all, nk, nv, sk, sv,
    meta, meta_s, len_s, par_s, owner_s, node_s,
    w_all, st_p, st_in, st_own, own_num, fac, ret, ret_in, fin_out, fin,
    loc_sem, meta_sem, ring_ss, ring_rs, a2a_ss, a2a_rs, x_ss, x_rs, m_ss, m_rs, st_ss, st_rs,
    ret_ss, ret_rs, fin_ss, fin_rs,
):
    r, k = lax.axis_index("req"), lax.axis_index("kv")
    x, z = r // nz, r % nz
    half = nz // 2
    hdp = HD // PIECES
    rows2 = 2 * STEPS

    def at_z(d):
        return (x * nz + (z + d + nz) % nz, k)

    def at_x(d):
        return (((x + d) % NX) * nz + z, k)

    def at_k(o):
        return (r, (k + o) % nkv)

    def remote(src, dst, ss, rs, dev):
        return pltpu.make_async_remote_copy(
            src_ref=src, dst_ref=dst, send_sem=ss, recv_sem=rs, device_id=dev, device_id_type=MESH
        )

    local = [
        pltpu.make_async_copy(pk_hbm, k_all.at[z, 0 : 2 * BLK], loc_sem.at[0]),
        pltpu.make_async_copy(pv_hbm, v_nat, loc_sem.at[1]),
        pltpu.make_async_copy(par_hbm, par_s, loc_sem.at[2]),
        pltpu.make_async_copy(owner_hbm, owner_s, loc_sem.at[3]),
        pltpu.make_async_copy(node_hbm, node_s, loc_sem.at[4]),
        pltpu.make_async_copy(len_hbm, len_s, loc_sem.at[5]),
        pltpu.make_async_copy(
            q_hbm.at[:, pl.ds(pl.multiple_of(k * (GROUP * HD), HD), GROUP * HD)], q_all.at[x, k], loc_sem.at[6]
        ),
        pltpu.make_async_copy(nk_hbm.at[:, pl.ds(pl.multiple_of(k * HD, HD), HD)], nk.at[k], loc_sem.at[7]),
        pltpu.make_async_copy(nv_hbm.at[:, pl.ds(pl.multiple_of(k * HD, HD), HD)], nv.at[k], loc_sem.at[8]),
        pltpu.make_async_copy(sk_hbm, sk, loc_sem.at[9]),
        pltpu.make_async_copy(sv_hbm, sv, loc_sem.at[10]),
    ]
    for c in local:
        c.start()

    barrier = pltpu.get_barrier_semaphore()
    peers = [at_z(1), at_z(-1)] + [at_x(d) for d in range(1, NX)] + [at_k(o) for o in range(1, nkv)]
    for dev in peers:
        pl.semaphore_signal(barrier, inc=1, device_id=dev, device_id_type=MESH)
    local[2].wait()
    flag = jnp.where(par_s[1] == 0, 0.0, LOW).astype(F32)
    k_all[z, 2 * BLK : 2 * BLK + FLAG] = jnp.full((FLAG, HD), flag, F32).astype(BF16)
    local[0].wait()
    pl.semaphore_wait(barrier, len(peers))

    tree = ring_tree(half)
    stage = {0: 0}
    for d in range(1, half + 1):
        stage[d] = stage[tree[d]] + 1
    depth = max(stage.values())
    kc = BLK

    def k_chunk(lo, hi):
        return lambda b, part: k_all.at[b, lo:hi]

    def v_chunk(p):
        def at(b, part):
            if part is None:
                return v_all[p].at[b]
            return v_all[p].at[b, part * (hdp // 2) : (part + 1) * (hdp // 2)]

        return at

    chunks = [(0, k_chunk(0, kc), 0), (1, k_chunk(kc, 2 * BLK + FLAG), 0)]
    chunks += [(2 + p, v_chunk(p), LAGS[p]) for p in range(PIECES)]

    def carried(c, dirn, d):
        if d < half:
            return True, None
        if c < 2:
            return c == dirn, None
        return True, dirn

    def hand_on(c, at, d, dirn):
        sign = 1 - 2 * dirn
        block = (z - sign * d + nz) % nz
        for e in sorted((e for e in tree if tree[e] == d), reverse=True):
            ok, part = carried(c, dirn, e)
            if ok:
                ref = at(block, part)
                remote(ref, ref, ring_ss.at[dirn, c, e], ring_rs.at[dirn, c, e], at_z(sign * (e - d))).start()

    def arrive(c, at, d, dirn):
        sign = 1 - 2 * dirn
        ok, part = carried(c, dirn, d)
        if ok:
            ref = at((z - sign * d + nz) % nz, part)
            remote(ref, ref, ring_ss.at[dirn, c, d], ring_rs.at[dirn, c, d], at_z(sign)).wait_recv()

    def slot(t):
        for c, at, lag in chunks:
            for d in range(half + 1):
                if lag + stage[d] != t:
                    continue
                for dirn in (0, 1):
                    if d > 0:
                        arrive(c, at, d, dirn)
                    hand_on(c, at, d, dirn)

    def drain():
        for c, at, lag in chunks:
            for d in range(1, half + 1):
                for dirn in (0, 1):
                    ok, part = carried(c, dirn, d)
                    if ok:
                        ref = at((z - (1 - 2 * dirn) * tree[d] + nz) % nz, part)
                        remote(ref, ref, ring_ss.at[dirn, c, d], ring_rs.at[dirn, c, d], at_z(1)).wait_send()

    def a2a(i, o, got=False):
        to = (k + o) % nkv
        frm = (k + nkv - o) % nkv
        wide = pl.ds(pl.multiple_of(to * (GROUP * HD), HD), GROUP * HD)
        thin = pl.ds(pl.multiple_of(to * HD, HD), HD)
        src = (q_hbm.at[:, wide], nk_hbm.at[:, thin], nv_hbm.at[:, thin])[i]
        dst = (q_all.at[x], nk, nv)[i]
        if got:
            src, dst = dst.at[frm], dst.at[frm]
        else:
            dst = dst.at[k]
        return remote(src, dst, a2a_ss.at[i, o], a2a_rs.at[i, o], at_k(o))

    slot(0)
    for i in range(3):
        for o in range(1, nkv):
            a2a(i, o).start()

    local[3].wait()
    local[4].wait()
    local[5].wait()
    lane = lax.broadcasted_iota(I32, (1, HD), 1)
    own_z = own_x = nodes = jnp.zeros((1, HD), I32)
    for i in range(2 * nkv):
        own_z = jnp.where(lane == i, owner_s[i] % nz, own_z)
        own_x = jnp.where(lane == i, owner_s[i] // nz, own_x)
        nodes = jnp.where(lane == i, node_s[i], nodes)
    pad = jnp.zeros((5, HD), I32)
    meta[x] = jnp.concatenate([own_z, own_x, nodes, pad], axis=0)
    for d in range(1, NX):
        remote(meta.at[x], meta.at[x], m_ss.at[d], m_rs.at[d], at_x(d)).start()

    local[1].wait()
    v_t = v_nat[...].astype(F32).T.astype(BF16)
    for p in range(PIECES):
        v_all[p][z] = v_t[p * hdp : (p + 1) * hdp]

    first = (lane // STEPS) % 2 == 0

    def both(a, b):
        return jnp.where(first, a, b)

    def pair_queries(src, p):
        slab = q_all[src, p]
        return jnp.concatenate([slab[:, j * HD : (j + 1) * HD] for j in range(GROUP)], axis=0)

    def send_queries():
        for o in range(1, nkv):
            a2a(0, o, True).wait_recv()
        local[6].wait()
        for d in (1, 3, 2):
            remote(q_all.at[x], q_all.at[x], x_ss.at[d], x_rs.at[d], at_x(d)).start()

    def await_queries(d):
        src = (x + d) % NX
        remote(q_all.at[src], q_all.at[src], x_ss.at[NX - d], x_rs.at[NX - d], at_x(d)).wait_recv()

    def await_meta():
        for d in range(1, NX):
            src = (x + d) % NX
            remote(meta.at[src], meta.at[src], m_ss.at[NX - d], m_rs.at[NX - d], at_x(d)).wait_recv()
        c = pltpu.make_async_copy(meta, meta_s, meta_sem.at[0])
        c.start()
        c.wait()

    def await_own():
        for o in range(1, nkv):
            a2a(1, o, True).wait_recv()
            a2a(2, o, True).wait_recv()
        for i in (7, 8, 9, 10):
            local[i].wait()

    def own_pair(p):
        queries = pair_queries(x, p)
        len_a, len_b = len_s[2 * p], len_s[2 * p + 1]
        s_suf = both(dot(sk[2 * p], queries, NT), dot(sk[2 * p + 1], queries, NT))
        s_new = dot(nk[p], queries, NT)
        pos = lax.broadcasted_iota(I32, (SUF, HD), 0)
        s_suf = jnp.where(pos < both(len_a, len_b), s_suf, LOW)
        row = lax.broadcasted_iota(I32, (rows2, HD), 0)
        col = lax.broadcasted_iota(I32, (rows2, HD), 1)
        seen = (row // STEPS == (col // STEPS) % 2) & (row % STEPS <= col % STEPS)
        s_new = jnp.where(seen, s_new, LOW)
        peak = jnp.maximum(jnp.max(s_suf, axis=0, keepdims=True), jnp.max(s_new, axis=0, keepdims=True))
        w_suf = jnp.exp2((s_suf - peak) * EXPO)
        w_new = jnp.exp2((s_new - peak) * EXPO)
        total = jnp.sum(w_suf, axis=0, keepdims=True) + jnp.sum(w_new, axis=0, keepdims=True)
        w_suf, w_new = w_suf.astype(BF16), w_new.astype(BF16)
        va = sv[2 * p].astype(F32).T.astype(BF16)
        vb = sv[2 * p + 1].astype(F32).T.astype(BF16)
        vn = nv[p].astype(F32).T.astype(BF16)
        own_num[p] = both(dot(va, w_suf), dot(vb, w_suf)) + dot(vn, w_new)
        st_own[0, p : p + 1] = peak
        st_own[1, p : p + 1] = total

    def prompt_weights(d, p):
        src = (x + d) % NX
        a, b = 2 * p, 2 * p + 1
        queries = pair_queries(src, p)
        ka, kb = meta_s[src, 0, a], meta_s[src, 0, b]
        node_a, node_b = meta_s[src, 2, a], meta_s[src, 2, b]
        s = both(dot(k_all[ka, 0 : 2 * BLK], queries, NT), dot(k_all[kb, 0 : 2 * BLK], queries, NT))
        flag_a = k_all[ka, 2 * BLK : 2 * BLK + FLAG].astype(F32)[0:1]
        flag_b = k_all[kb, 2 * BLK : 2 * BLK + FLAG].astype(F32)[0:1]
        nodes_ab = both(node_a, node_b)
        s0 = s[0:BLK] + jnp.where(nodes_ab == 1, both(flag_a, flag_b), 0.0)
        s1 = s[BLK:] + jnp.where(nodes_ab == 1, 0.0, LOW)
        peak = jnp.max(jnp.maximum(s0, s1), axis=0, keepdims=True)
        w0 = jnp.exp2((s0 - peak) * EXPO)
        w1 = jnp.exp2((s1 - peak) * EXPO)
        st_p[d, 0, p : p + 1] = peak
        st_p[d, 1, p : p + 1] = jnp.sum(w0 + w1, axis=0, keepdims=True)
        w_all[d, p, 0:BLK] = w0.astype(BF16)
        w_all[d, p, BLK:] = w1.astype(BF16)

    def send_stats(d):
        e = NX - d
        remote(st_p.at[d], st_in.at[e], st_ss.at[d], st_rs.at[e], at_x(d)).start()

    def prompt_values(piece, d, p):
        src = (x + d) % NX
        va = v_all[piece][meta_s[src, 0, 2 * p]]
        vb = v_all[piece][meta_s[src, 0, 2 * p + 1]]
        w = w_all[d, p]
        ret[piece, d, p] = both(dot(va, w), dot(vb, w)).astype(BF16)

    def send_back(piece, d):
        e = NX - d
        remote(
            ret.at[piece, d], ret_in.at[piece, e], ret_ss.at[piece, d], ret_rs.at[piece, e], at_x(d)
        ).start()

    def await_back(piece):
        for e in range(1, NX):
            remote(
                ret_in.at[piece, e], ret_in.at[piece, e], ret_ss.at[piece, e], ret_rs.at[piece, e], at_x(e)
            ).wait_recv()

    def owner_side(p):
        xa, xb = meta_s[x, 1, 2 * p], meta_s[x, 1, 2 * p + 1]
        return both((xa - x + NX) % NX, (xb - x + NX) % NX)

    def factors():
        for e in range(1, NX):
            remote(st_in.at[e], st_in.at[e], st_ss.at[e], st_rs.at[e], at_x(e)).wait_recv()
        for p in range(nkv):
            side = owner_side(p)
            peak, total = st_p[0, 0, p : p + 1], st_p[0, 1, p : p + 1]
            for e in range(1, NX):
                peak = jnp.where(side == e, st_in[e, 0, p : p + 1], peak)
                total = jnp.where(side == e, st_in[e, 1, p : p + 1], total)
            peak_own, total_own = st_own[0, p : p + 1], st_own[1, p : p + 1]
            top = jnp.maximum(peak, peak_own)
            f_p = jnp.exp2((peak - top) * EXPO)
            f_o = jnp.exp2((peak_own - top) * EXPO)
            inv = 1.0 / (f_p * total + f_o * total_own)
            fac[0, p : p + 1] = f_p * inv
            fac[1, p : p + 1] = f_o * inv

    def merge(piece, p):
        side = owner_side(p)
        num = ret[piece, 0, p].astype(F32)
        for e in range(1, NX):
            num = jnp.where(side == e, ret_in[piece, e, p].astype(F32), num)
        own = own_num[p, piece * hdp : (piece + 1) * hdp]
        fin_out[piece, p] = (num * fac[0, p : p + 1] + own * fac[1, p : p + 1]).astype(BF16)

    def send_final(piece):
        for o in range(1, nkv):
            to = (k + o) % nkv
            remote(
                fin_out.at[piece, to], fin.at[piece, k], fin_ss.at[piece, o], fin_rs.at[piece, o], at_k(o)
            ).start()
        fin[piece, k] = fin_out[piece, k]

    scores = [(d, p) for d in (0, 1, 3, 2) for p in range(nkv)]
    before = {t: [] for t in range(1, LAGS[-1] + depth + 1)}

    def plan(t, f, *args):
        before[min(max(t, 1), LAGS[-1] + depth)].append(functools.partial(f, *args))

    plan(2, send_queries)
    plan(3, await_own)
    for p in range(nkv):
        plan(3 + (p * 3) // nkv, own_pair, p)
    plan(min(6, depth + 1), await_meta)
    late = []
    k_done = depth + 1
    v0_done = LAGS[0] + depth + 1
    gap = max(v0_done - k_done, 1)
    for i, (d, p) in enumerate(scores):
        t = k_done + (i * gap) // len(scores)
        if p == 0 and d:
            plan(t, await_queries, d)
        plan(t, prompt_weights, d, p)
        if p == nkv - 1 and d:
            plan(t, send_stats, d)
    values = [(d, p) for d in (2, 1, 3, 0) for p in range(nkv)]
    gap = LAGS[1] - LAGS[0]
    for i, (d, p) in enumerate(values):
        t = v0_done + (i * gap) // len(values)
        plan(t, prompt_values, 0, d, p)
        if p == nkv - 1 and d:
            plan(t, send_back, 0, d)

    for t in range(1, LAGS[-1] + depth + 1):
        for f in before[t]:
            f()
        slot(t)
    for d, p in values:
        prompt_values(1, d, p)
        if p == nkv - 1 and d:
            send_back(1, d)
    factors()
    for piece in range(PIECES):
        await_back(piece)
        for p in range(nkv):
            merge(piece, p)
        send_final(piece)
    for piece in range(PIECES):
        for o in range(1, nkv):
            frm = (k + nkv - o) % nkv
            remote(
                fin.at[piece, frm], fin.at[piece, frm], fin_ss.at[piece, o], fin_rs.at[piece, o], at_k(o)
            ).wait_recv()
    for g in range(nkv):
        rows = jnp.concatenate([fin[piece, g].astype(F32) for piece in range(PIECES)], axis=0)
        rows = rows.T.astype(BF16)
        for j in range(GROUP):
            out_ref[:, (g * GROUP + j) * HD : (g * GROUP + j + 1) * HD] = rows[j * rows2 : (j + 1) * rows2]

    drain()
    for o in range(1, nkv):
        for i in range(3):
            a2a(i, o).wait_send()
        for piece in range(PIECES):
            remote(
                fin_out.at[piece, 0], fin.at[piece, 0], fin_ss.at[piece, o], fin_rs.at[piece, o], at_k(o)
            ).wait_send()
    for d in range(1, NX):
        remote(q_all.at[x], q_all.at[x], x_ss.at[d], x_rs.at[d], at_x(d)).wait_send()
        remote(meta.at[x], meta.at[x], m_ss.at[d], m_rs.at[d], at_x(d)).wait_send()
        remote(st_p.at[d], st_in.at[d], st_ss.at[d], st_rs.at[d], at_x(d)).wait_send()
        for piece in range(PIECES):
            remote(
                ret.at[piece, d], ret_in.at[piece, d], ret_ss.at[piece, d], ret_rs.at[piece, d], at_x(d)
            ).wait_send()


def solution(mesh):
    nz = mesh.shape["req"] // NX
    nkv = mesh.shape["kv"]
    half = nz // 2
    hdp = HD // PIECES
    rows2 = 2 * STEPS

    def shards(q, nk, nv, sk, sv, length, pk, pv, parent, owner, node):
        q = q.reshape(rows2, -1)
        nk = nk.reshape(rows2, -1)
        nv = nv.reshape(rows2, -1)
        pk = pk.reshape(2 * BLK, HD)
        pv = pv.reshape(2 * BLK, HD)
        dma = pltpu.SemaphoreType.DMA
        vmem = pltpu.VMEM
        out = pl.pallas_call(
            functools.partial(kernel, nz, nkv),
            out_shape=jax.ShapeDtypeStruct((rows2, nkv * GROUP * HD), BF16),
            in_specs=[pl.BlockSpec(memory_space=pl.ANY)] * 11,
            out_specs=pl.BlockSpec(memory_space=pltpu.VMEM),
            scratch_shapes=[
                vmem((nz, 2 * BLK + FLAG, HD), BF16),
                vmem((2 * BLK, HD), BF16),
                [vmem((nz, hdp, 2 * BLK), BF16)] * PIECES,
                vmem((NX, nkv, rows2, GROUP * HD), BF16),
                vmem((nkv, rows2, HD), BF16),
                vmem((nkv, rows2, HD), BF16),
                vmem((2 * nkv, SUF, HD), BF16),
                vmem((2 * nkv, SUF, HD), BF16),
                vmem((NX, 8, HD), I32),
                pltpu.SMEM((NX, 8, HD), I32),
                pltpu.SMEM((2 * nkv,), I32),
                pltpu.SMEM((2,), I32),
                pltpu.SMEM((2 * nkv,), I32),
                pltpu.SMEM((2 * nkv,), I32),
                vmem((NX, nkv, 2 * BLK, HD), BF16),
                vmem((NX, 2, nkv, HD), F32),
                vmem((NX, 2, nkv, HD), F32),
                vmem((2, nkv, HD), F32),
                vmem((nkv, HD, HD), F32),
                vmem((2, nkv, HD), F32),
                vmem((PIECES, NX, nkv, hdp, HD), BF16),
                vmem((PIECES, NX, nkv, hdp, HD), BF16),
                vmem((PIECES, nkv, hdp, HD), BF16),
                vmem((PIECES, nkv, hdp, HD), BF16),
                dma((11,)),
                dma((1,)),
                dma((2, 2 + PIECES, half + 1)),
                dma((2, 2 + PIECES, half + 1)),
                dma((3, nkv)),
                dma((3, nkv)),
                dma((NX,)),
                dma((NX,)),
                dma((NX,)),
                dma((NX,)),
                dma((NX,)),
                dma((NX,)),
                dma((PIECES, NX)),
                dma((PIECES, NX)),
                dma((PIECES, nkv)),
                dma((PIECES, nkv)),
            ],
            compiler_params=pltpu.CompilerParams(
                collective_id=0, has_side_effects=True, vmem_limit_bytes=32 * 2**20
            ),
        )(q, nk, nv, sk, sv, pk, pv, length, parent, owner, node)
        return out.reshape(2, STEPS, -1)

    in_specs = (
        P(("req", "kv"), None, None),
        P(("req", "kv"), None, None),
        P(("req", "kv"), None, None),
        P("req", None, "kv"),
        P("req", None, "kv"),
        P("req"),
        P("req", None, "kv"),
        P("req", None, "kv"),
        P("req"),
        P("req"),
        P("req"),
    )
    return jax.shard_map(
        shards, mesh=mesh, in_specs=in_specs, out_specs=P(("req", "kv"), None, None), check_vma=False
    )
```

```python
import functools
import math

import jax
import jax.numpy as jnp
from jax import lax
from jax.experimental import pallas as pl
from jax.experimental.pallas import tpu as pltpu
from jax.sharding import PartitionSpec as P

MESH = pl.DeviceIdType.MESH
BF16, F32, I32 = jnp.bfloat16, jnp.float32, jnp.int32

HD = 128
BLK = 128
STEPS = 8
GROUP = 8
SUF = 64
NX = 4
FLAG = 16
LOW = -1e30
EXPO = math.log2(math.e) / math.sqrt(HD)

NN = (((1,), (0,)), ((), ()))
NT = (((1,), (1,)), ((), ()))


def dot(a, b, dims=NN):
    return lax.dot_general(a, b, dims, preferred_element_type=F32)


def block_tree(half, jumps):
    tree = {d: d - 1 for d in range(1, half + 1)}
    tree.update({d: frm for d, frm in jumps.items() if d <= half})
    stage = {0: 0}
    while len(stage) <= half:
        stage.update({d: stage[frm] + 1 for d, frm in tree.items() if frm in stage})
    return tree, stage


LAGS = (0, 0)
JUMPS = ({8: 6}, {})


def kernel(
    nz, nkv,
    q_hbm, nk_hbm, nv_hbm, sk_hbm, sv_hbm, pk_hbm, pv_hbm, len_hbm, par_hbm, owner_hbm, node_hbm,
    fin,
    k_all, v_nat, v_all, q_all, nk, nv, sk, sv,
    meta, meta_s, len_s, par_s, owner_s, node_s,
    w_all, st_p, st_in, st_own, own_num, fac, ret, relay, ret_in, fin_out,
    loc_sem, meta_sem, ring_ss, ring_rs, a2a_ss, a2a_rs, x_ss, x_rs, m_ss, m_rs, st_ss, st_rs,
    ret_ss, ret_rs, fin_ss, fin_rs,
):
    r, k = lax.axis_index("req"), lax.axis_index("kv")
    x, z = r // nz, r % nz
    half = nz // 2
    rows2 = 2 * STEPS
    mid = nkv // 2
    sub = max(mid // 2, 1)
    parts = mid // sub

    def pair(i):
        return (k + 1 + i) % nkv

    def at_z(d):
        return (x * nz + (z + d + nz) % nz, k)

    def at_x(d):
        return (((x + d) % NX) * nz + z, k)

    def at_k(o):
        return (r, (k + o) % nkv)

    def remote(src, dst, ss, rs, dev):
        return pltpu.make_async_remote_copy(
            src_ref=src, dst_ref=dst, send_sem=ss, recv_sem=rs, device_id=dev, device_id_type=MESH
        )

    local = [
        pltpu.make_async_copy(pk_hbm, k_all.at[z, 0 : 2 * BLK], loc_sem.at[0]),
        pltpu.make_async_copy(pv_hbm, v_nat, loc_sem.at[1]),
        pltpu.make_async_copy(par_hbm, par_s, loc_sem.at[2]),
        pltpu.make_async_copy(owner_hbm, owner_s, loc_sem.at[3]),
        pltpu.make_async_copy(node_hbm, node_s, loc_sem.at[4]),
        pltpu.make_async_copy(len_hbm, len_s, loc_sem.at[5]),
        pltpu.make_async_copy(
            q_hbm.at[:, pl.ds(pl.multiple_of(k * (GROUP * HD), HD), GROUP * HD)], q_all.at[x, k], loc_sem.at[6]
        ),
        pltpu.make_async_copy(nk_hbm.at[:, pl.ds(pl.multiple_of(k * HD, HD), HD)], nk.at[k], loc_sem.at[7]),
        pltpu.make_async_copy(nv_hbm.at[:, pl.ds(pl.multiple_of(k * HD, HD), HD)], nv.at[k], loc_sem.at[8]),
        pltpu.make_async_copy(sk_hbm, sk, loc_sem.at[9]),
        pltpu.make_async_copy(sv_hbm, sv, loc_sem.at[10]),
    ]
    for c in local:
        c.start()

    barrier = pltpu.get_barrier_semaphore()
    trees = [block_tree(half, j) for j in JUMPS]
    jumps = sorted({abs(e - d) for tree, _ in trees for e, d in tree.items()})
    peers = [at_z(s * d) for d in jumps for s in (1, -1)] + [at_x(d) for d in range(1, NX)] + [at_k(o) for o in range(1, nkv)]
    for dev in peers:
        pl.semaphore_signal(barrier, inc=1, device_id=dev, device_id_type=MESH)
    local[2].wait()
    flag = jnp.where(par_s[1] == 0, 0.0, LOW).astype(F32)
    k_all[z, 2 * BLK : 2 * BLK + FLAG] = jnp.full((FLAG, HD), flag, F32).astype(BF16)
    local[0].wait()
    pl.semaphore_wait(barrier, len(peers))

    done = [lag + max(stage.values()) + 1 for lag, (_, stage) in zip(LAGS, trees)]
    def chunk(ref, lo, hi):
        return lambda b: ref.at[b, lo:hi]

    chunks = [
        (0, chunk(k_all, 0, BLK), 0),
        (1, chunk(k_all, BLK, 2 * BLK + FLAG), 0),
        (2, chunk(v_all, 0, HD // 2), 1),
        (3, chunk(v_all, HD // 2, HD), 1),
    ]

    def carried(c, dirn, d):
        return d < half or c % 2 == dirn

    def hand_on(c, at, tree, d, dirn):
        sign = 1 - 2 * dirn
        block = (z - sign * d + nz) % nz
        for e in sorted((e for e in tree if tree[e] == d), reverse=True):
            if carried(c, dirn, e):
                ref = at(block)
                remote(ref, ref, ring_ss.at[dirn, c, e], ring_rs.at[dirn, c, e], at_z(sign * (e - d))).start()

    def arrive(c, at, d, dirn):
        sign = 1 - 2 * dirn
        if carried(c, dirn, d):
            ref = at((z - sign * d + nz) % nz)
            remote(ref, ref, ring_ss.at[dirn, c, d], ring_rs.at[dirn, c, d], at_z(sign)).wait_recv()

    def slot(t, *kinds):
        for c, at, i in chunks:
            if kinds and i not in kinds:
                continue
            tree, stage = trees[i]
            for d in range(half + 1):
                if LAGS[i] + stage[d] != t:
                    continue
                for dirn in (0, 1):
                    if d > 0:
                        arrive(c, at, d, dirn)
                    hand_on(c, at, tree, d, dirn)

    def drain():
        for c, at, i in chunks:
            tree = trees[i][0]
            for d in range(1, half + 1):
                for dirn in (0, 1):
                    if carried(c, dirn, d):
                        ref = at((z - (1 - 2 * dirn) * tree[d] + nz) % nz)
                        remote(ref, ref, ring_ss.at[dirn, c, d], ring_rs.at[dirn, c, d], at_z(1)).wait_send()

    def a2a(i, o, got=False):
        to = (k + o) % nkv
        frm = (k + nkv - o) % nkv
        wide = pl.ds(pl.multiple_of(to * (GROUP * HD), HD), GROUP * HD)
        thin = pl.ds(pl.multiple_of(to * HD, HD), HD)
        src = (q_hbm.at[:, wide], nk_hbm.at[:, thin], nv_hbm.at[:, thin])[i]
        dst = (q_all.at[x], nk, nv)[i]
        if got:
            src, dst = dst.at[frm], dst.at[frm]
        else:
            dst = dst.at[k]
        return remote(src, dst, a2a_ss.at[i, o], a2a_rs.at[i, o], at_k(o))

    slot(0, 0)
    for i in range(3):
        for o in range(1, nkv):
            a2a(i, o).start()

    local[1].wait()
    v_all[z] = v_nat[...].astype(F32).T.astype(BF16)
    slot(0, 1)

    local[3].wait()
    local[4].wait()
    local[5].wait()
    lane = lax.broadcasted_iota(I32, (1, HD), 1)
    own_z = own_x = nodes = jnp.zeros((1, HD), I32)
    for i in range(2 * nkv):
        own_z = jnp.where(lane == i, owner_s[i] % nz, own_z)
        own_x = jnp.where(lane == i, owner_s[i] // nz, own_x)
        nodes = jnp.where(lane == i, node_s[i], nodes)
    pad = jnp.zeros((5, HD), I32)
    meta[x] = jnp.concatenate([own_z, own_x, nodes, pad], axis=0)
    for d in range(1, NX):
        remote(meta.at[x], meta.at[x], m_ss.at[d], m_rs.at[d], at_x(d)).start()

    first = (lane // STEPS) % 2 == 0

    def both(a, b):
        return jnp.where(first, a, b)

    def pair_queries(src, p):
        slab = q_all[src, p]
        return jnp.concatenate([slab[:, j * HD : (j + 1) * HD] for j in range(GROUP)], axis=0)

    def send_queries():
        for o in range(1, nkv):
            a2a(0, o, True).wait_recv()
        local[6].wait()
        for d in (1, 3, 2):
            remote(q_all.at[x], q_all.at[x], x_ss.at[d], x_rs.at[d], at_x(d)).start()

    def await_queries(d):
        src = (x + d) % NX
        remote(q_all.at[src], q_all.at[src], x_ss.at[NX - d], x_rs.at[NX - d], at_x(d)).wait_recv()

    def await_meta():
        for d in range(1, NX):
            src = (x + d) % NX
            remote(meta.at[src], meta.at[src], m_ss.at[NX - d], m_rs.at[NX - d], at_x(d)).wait_recv()
        c = pltpu.make_async_copy(meta, meta_s, meta_sem.at[0])
        c.start()
        c.wait()

    def await_own():
        for o in range(1, nkv):
            a2a(1, o, True).wait_recv()
            a2a(2, o, True).wait_recv()
        for i in (7, 8, 9, 10):
            local[i].wait()

    def own_pair(i):
        p = pair(i)
        queries = pair_queries(x, p)
        len_a, len_b = len_s[2 * p], len_s[2 * p + 1]
        s_suf = both(dot(sk[2 * p], queries, NT), dot(sk[2 * p + 1], queries, NT))
        s_new = dot(nk[p], queries, NT)
        pos = lax.broadcasted_iota(I32, (SUF, HD), 0)
        s_suf = jnp.where(pos < both(len_a, len_b), s_suf, LOW)
        row = lax.broadcasted_iota(I32, (rows2, HD), 0)
        col = lax.broadcasted_iota(I32, (rows2, HD), 1)
        seen = (row // STEPS == (col // STEPS) % 2) & (row % STEPS <= col % STEPS)
        s_new = jnp.where(seen, s_new, LOW)
        peak = jnp.maximum(jnp.max(s_suf, axis=0, keepdims=True), jnp.max(s_new, axis=0, keepdims=True))
        w_suf = jnp.exp2((s_suf - peak) * EXPO)
        w_new = jnp.exp2((s_new - peak) * EXPO)
        total = jnp.sum(w_suf, axis=0, keepdims=True) + jnp.sum(w_new, axis=0, keepdims=True)
        w_suf, w_new = w_suf.astype(BF16), w_new.astype(BF16)
        va = sv[2 * p].astype(F32).T.astype(BF16)
        vb = sv[2 * p + 1].astype(F32).T.astype(BF16)
        vn = nv[p].astype(F32).T.astype(BF16)
        own_num[i] = both(dot(va, w_suf), dot(vb, w_suf)) + dot(vn, w_new)
        st_own[0, i : i + 1] = peak
        st_own[1, i : i + 1] = total

    def prompt_weights(d, i):
        src, p = (x + d) % NX, pair(i)
        a, b = 2 * p, 2 * p + 1
        queries = pair_queries(src, p)
        ka, kb = meta_s[src, 0, a], meta_s[src, 0, b]
        node_a, node_b = meta_s[src, 2, a], meta_s[src, 2, b]
        s = both(dot(k_all[ka, 0 : 2 * BLK], queries, NT), dot(k_all[kb, 0 : 2 * BLK], queries, NT))
        flag_a = k_all[ka, 2 * BLK : 2 * BLK + FLAG].astype(F32)[0:1]
        flag_b = k_all[kb, 2 * BLK : 2 * BLK + FLAG].astype(F32)[0:1]
        nodes_ab = both(node_a, node_b)
        s0 = s[0:BLK] + jnp.where(nodes_ab == 1, both(flag_a, flag_b), 0.0)
        s1 = s[BLK:] + jnp.where(nodes_ab == 1, 0.0, LOW)
        peak = jnp.max(jnp.maximum(s0, s1), axis=0, keepdims=True)
        w0 = jnp.exp2((s0 - peak) * EXPO)
        w1 = jnp.exp2((s1 - peak) * EXPO)
        st_p[d, 0, i : i + 1] = peak
        st_p[d, 1, i : i + 1] = jnp.sum(w0 + w1, axis=0, keepdims=True)
        w_all[d, i, 0:BLK] = w0.astype(BF16)
        w_all[d, i, BLK:] = w1.astype(BF16)

    def send_stats(d):
        e = NX - d
        remote(st_p.at[d], st_in.at[e], st_ss.at[d], st_rs.at[e], at_x(d)).start()

    def prompt_values(d, i):
        src, p = (x + d) % NX, pair(i)
        w = w_all[d, i]
        num = both(dot(v_all[meta_s[src, 0, 2 * p]], w), dot(v_all[meta_s[src, 0, 2 * p + 1]], w))
        ret[d, i] = num.astype(BF16)

    def owner_side(src, i):
        p = pair(i)
        return both((meta_s[src, 1, 2 * p] - x + NX) % NX, (meta_s[src, 1, 2 * p + 1] - x + NX) % NX)

    def places(high, s):
        lo = high * mid + s * sub
        return slice(lo, lo + sub)

    routes = [
        (lambda s: ret.at[2, places(0, s)], lambda s: relay.at[0, s * sub : (s + 1) * sub], -1),
        (lambda s: ret.at[2, places(1, s)], lambda s: relay.at[1, s * sub : (s + 1) * sub], 1),
        (lambda s: ret.at[3, places(1, s)], lambda s: ret_in.at[0, places(1, s)], -1),
        (lambda s: ret.at[1, places(0, s)], lambda s: ret_in.at[1, places(0, s)], 1),
        (lambda s: ret.at[3, places(0, s)], lambda s: ret_in.at[0, places(0, s)], -1),
        (lambda s: ret.at[1, places(1, s)], lambda s: ret_in.at[1, places(1, s)], 1),
    ]

    def back(n, s):
        src, dst, step = routes[n]
        return remote(src(s), dst(s), ret_ss.at[n, s], ret_rs.at[n, s], at_x(step + NX))

    def arrived(n, s):
        dst = routes[n][1](s)
        remote(dst, dst, ret_ss.at[n, s], ret_rs.at[n, s], at_x(1)).wait_recv()

    def put_between(high, s):
        d, far = (1, 3) if high else (3, 1)
        for i in range(nkv)[places(high, s)]:
            there = owner_side((x + d) % NX, i) == far
            ret[d, i] = jnp.where(there, relay[high, i - high * mid].astype(F32), ret[d, i].astype(F32)).astype(BF16)

    def factors():
        for e in range(1, NX):
            remote(st_in.at[e], st_in.at[e], st_ss.at[e], st_rs.at[e], at_x(e)).wait_recv()
        for i in range(nkv):
            side = owner_side(x, i)
            row = slice(i, i + 1)
            peak, total = st_p[0, 0, row], st_p[0, 1, row]
            for e in range(1, NX):
                peak = jnp.where(side == e, st_in[e, 0, row], peak)
                total = jnp.where(side == e, st_in[e, 1, row], total)
            peak_own, total_own = st_own[0, row], st_own[1, row]
            top = jnp.maximum(peak, peak_own)
            f_p = jnp.exp2((peak - top) * EXPO)
            f_o = jnp.exp2((peak_own - top) * EXPO)
            inv = 1.0 / (f_p * total + f_o * total_own)
            fac[0, row] = f_p * inv
            fac[1, row] = f_o * inv

    def merge(i):
        side = owner_side(x, i)
        right = (side == 1) | (side == 2) if i < mid else side == 1
        num = jnp.where(right, ret_in[0, i].astype(F32), ret_in[1, i].astype(F32))
        num = jnp.where(side == 0, ret[0, i].astype(F32), num)
        out = num * fac[0, i : i + 1] + own_num[i] * fac[1, i : i + 1]
        fin_out[i] = out.astype(BF16)
        if i < nkv - 1:
            remote(fin_out.at[i], fin.at[k], fin_ss.at[i], fin_rs.at[i], (r, pair(i))).start()
        else:
            pltpu.make_async_copy(fin_out.at[i], fin.at[k], meta_sem.at[0]).start()

    def final(i):
        g = (k + 2 * nkv - 1 - i) % nkv
        remote(fin.at[g], fin.at[g], fin_ss.at[i], fin_rs.at[i], at_k(1)).wait_recv()

    last = max(done)
    before = {t: [] for t in range(1, last + 1)}

    def plan(t, f, *args):
        before[min(t, last)].append(functools.partial(f, *args))

    plan(2, send_queries)
    plan(3, await_own)
    for p in range(nkv):
        plan(3 + (p * 3) // nkv, own_pair, p)
    plan(min(6, done[0]), await_meta)

    def spread(work, start, end):
        for i, (d, p) in enumerate(work):
            t = start + (i * max(end - start, 1)) // len(work)
            yield t, d, p

    order = [(d, p) for d in (0, 1, 3, 2) for p in range(nkv)]
    for t, d, p in spread(order, done[0], done[1]):
        if p == 0 and d:
            plan(t, await_queries, d)
        plan(t, prompt_weights, d, p)
        if p == nkv - 1 and d:
            plan(t, send_stats, d)
    for t in range(1, last + 1):
        for f in before[t]:
            f()
        if t < last:
            slot(t)

    ways = [(high, s) for s in range(parts) for high in (0, 1)]
    for high, s in ways:
        for i in range(nkv)[places(high, s)]:
            prompt_values(2, i)
        back(high, s).start()
    for high, s in ways:
        d = 3 if high else 1
        for i in range(nkv)[places(high, s)]:
            prompt_values(d, i)
        back(2 if high else 3, s).start()
    for high, s in ways:
        d = 1 if high else 3
        for i in range(nkv)[places(high, s)]:
            prompt_values(d, i)
    for i in range(nkv):
        prompt_values(0, i)
    for high, s in ways:
        arrived(high, s)
        put_between(high, s)
        back(4 + high, s).start()
    factors()
    for high, s in ways:
        arrived(2 if high else 3, s)
    for high, s in ways:
        arrived(4 + high, s)
        for i in range(nkv)[places(high, s)]:
            merge(i)
    for high, s in ways:
        for i in range(nkv)[places(high, s)]:
            if i < nkv - 1:
                final(i)

    pltpu.make_async_copy(fin_out.at[nkv - 1], fin.at[k], meta_sem.at[0]).wait()

    drain()
    for o in range(1, nkv):
        for i in range(3):
            a2a(i, o).wait_send()
    for i in range(nkv - 1):
        remote(fin_out.at[i], fin.at[i], fin_ss.at[i], fin_rs.at[i], at_k(1)).wait_send()
    for d in range(1, NX):
        remote(q_all.at[x], q_all.at[x], x_ss.at[d], x_rs.at[d], at_x(d)).wait_send()
        remote(meta.at[x], meta.at[x], m_ss.at[d], m_rs.at[d], at_x(d)).wait_send()
        remote(st_p.at[d], st_in.at[d], st_ss.at[d], st_rs.at[d], at_x(d)).wait_send()
    for n in range(len(routes)):
        for s in range(parts):
            back(n, s).wait_send()


def finish(fin, out_ref):
    rows2 = 2 * STEPS
    for g in range(fin.shape[0]):
        rows = fin[g].astype(F32).T.astype(BF16)
        for j in range(GROUP):
            at = (g * GROUP + j) * HD
            out_ref[:, at : at + HD] = rows[j * rows2 : (j + 1) * rows2]


def solution(mesh):
    nz = mesh.shape["req"] // NX
    nkv = mesh.shape["kv"]
    half = nz // 2
    mid = nkv // 2
    parts = mid // max(mid // 2, 1)
    rows2 = 2 * STEPS

    def shards(q, nk, nv, sk, sv, length, pk, pv, parent, owner, node):
        q = q.reshape(rows2, -1)
        nk = nk.reshape(rows2, -1)
        nv = nv.reshape(rows2, -1)
        pk = pk.reshape(2 * BLK, HD)
        pv = pv.reshape(2 * BLK, HD)
        dma = pltpu.SemaphoreType.DMA
        vmem = pltpu.VMEM
        out = pl.pallas_call(
            functools.partial(kernel, nz, nkv),
            out_shape=jax.ShapeDtypeStruct((nkv, HD, HD), BF16),
            in_specs=[pl.BlockSpec(memory_space=pltpu.HBM)] * 11,
            out_specs=pl.BlockSpec(memory_space=pltpu.HBM),
            scratch_shapes=[
                vmem((nz, 2 * BLK + FLAG, HD), BF16),
                vmem((2 * BLK, HD), BF16),
                vmem((nz, HD, 2 * BLK), BF16),
                vmem((NX, nkv, rows2, GROUP * HD), BF16),
                vmem((nkv, rows2, HD), BF16),
                vmem((nkv, rows2, HD), BF16),
                vmem((2 * nkv, SUF, HD), BF16),
                vmem((2 * nkv, SUF, HD), BF16),
                vmem((NX, 8, HD), I32),
                pltpu.SMEM((NX, 8, HD), I32),
                pltpu.SMEM((2 * nkv,), I32),
                pltpu.SMEM((2,), I32),
                pltpu.SMEM((2 * nkv,), I32),
                pltpu.SMEM((2 * nkv,), I32),
                vmem((NX, nkv, 2 * BLK, HD), BF16),
                vmem((NX, 2, nkv, HD), F32),
                vmem((NX, 2, nkv, HD), F32),
                vmem((2, nkv, HD), F32),
                vmem((nkv, HD, HD), F32),
                vmem((2, nkv, HD), F32),
                vmem((NX, nkv, HD, HD), BF16),
                vmem((2, mid, HD, HD), BF16),
                vmem((2, nkv, HD, HD), BF16),
                vmem((nkv, HD, HD), BF16),
                dma((11,)),
                dma((1,)),
                dma((2, 4, half + 1)),
                dma((2, 4, half + 1)),
                dma((3, nkv)),
                dma((3, nkv)),
                dma((NX,)),
                dma((NX,)),
                dma((NX,)),
                dma((NX,)),
                dma((NX,)),
                dma((NX,)),
                dma((6, parts)),
                dma((6, parts)),
                dma((nkv,)),
                dma((nkv,)),
            ],
            compiler_params=pltpu.CompilerParams(
                collective_id=0, has_side_effects=True, vmem_limit_bytes=60 * 2**20
            ),
        )(q, nk, nv, sk, sv, pk, pv, length, parent, owner, node)
        out = pl.pallas_call(
            finish,
            grid=(2,),
            in_specs=[pl.BlockSpec((nkv // 2, HD, HD), lambda i: (i, 0, 0))],
            out_specs=pl.BlockSpec((rows2, nkv // 2 * GROUP * HD), lambda i: (0, i)),
            out_shape=jax.ShapeDtypeStruct((rows2, nkv * GROUP * HD), BF16),
        )(out)
        return out.reshape(2, STEPS, -1)

    in_specs = (
        P(("req", "kv"), None, None),
        P(("req", "kv"), None, None),
        P(("req", "kv"), None, None),
        P("req", None, "kv"),
        P("req", None, "kv"),
        P("req"),
        P("req", None, "kv"),
        P("req", None, "kv"),
        P("req"),
        P("req"),
        P("req"),
    )
    return jax.shard_map(
        shards, mesh=mesh, in_specs=in_specs, out_specs=P(("req", "kv"), None, None), check_vma=False
    )
```

```python
import functools
import math

import jax
import jax.numpy as jnp
from jax import lax
from jax.experimental import pallas as pl
from jax.experimental.pallas import tpu as pltpu
from jax.sharding import PartitionSpec as P

MESH = pl.DeviceIdType.MESH
BF16, F32, I32 = jnp.bfloat16, jnp.float32, jnp.int32

HD = 128
BLK = 128
STEPS = 8
GROUP = 8
SUF = 64
NX = 4
FLAG = 16
LOW = -1e30
EXPO = math.log2(math.e) / math.sqrt(HD)

NN = (((1,), (0,)), ((), ()))
NT = (((1,), (1,)), ((), ()))


def dot(a, b, dims=NN):
    return lax.dot_general(a, b, dims, preferred_element_type=F32)


def block_tree(half, jumps):
    tree = {d: d - 1 for d in range(1, half + 1)}
    tree.update({d: frm for d, frm in jumps.items() if d <= half})
    stage = {0: 0}
    while len(stage) <= half:
        stage.update({d: stage[frm] + 1 for d, frm in tree.items() if frm in stage})
    return tree, stage


LAGS = (0, 0)
JUMPS = ({8: 6}, {})


def kernel(
    nz, nkv,
    q_hbm, nk_hbm, nv_hbm, sk_hbm, sv_hbm, pk_hbm, pv_hbm, len_hbm, par_hbm, owner_hbm, node_hbm,
    out_ref,
    k_all, v_nat, v_all, q_all, nk, nv, sk, sv,
    meta, meta_s, len_s, par_s, owner_s, node_s,
    w_all, st_p, st_in, st_own, own_num, fac, ret, relay, ret_in, fin_out, fin,
    loc_sem, meta_sem, ring_ss, ring_rs, a2a_ss, a2a_rs, x_ss, x_rs, m_ss, m_rs, st_ss, st_rs,
    ret_ss, ret_rs, fin_ss, fin_rs,
):
    r, k = lax.axis_index("req"), lax.axis_index("kv")
    x, z = r // nz, r % nz
    half = nz // 2
    rows2 = 2 * STEPS
    mid = nkv // 2
    sub = max(mid // 4, 1)
    parts = mid // sub

    def pair(i):
        return (k + 1 + i) % nkv

    def at_z(d):
        return (x * nz + (z + d + nz) % nz, k)

    def at_x(d):
        return (((x + d) % NX) * nz + z, k)

    def at_k(o):
        return (r, (k + o) % nkv)

    def remote(src, dst, ss, rs, dev):
        return pltpu.make_async_remote_copy(
            src_ref=src, dst_ref=dst, send_sem=ss, recv_sem=rs, device_id=dev, device_id_type=MESH
        )

    local = [
        pltpu.make_async_copy(pk_hbm, k_all.at[z, 0 : 2 * BLK], loc_sem.at[0]),
        pltpu.make_async_copy(pv_hbm, v_nat, loc_sem.at[1]),
        pltpu.make_async_copy(par_hbm, par_s, loc_sem.at[2]),
        pltpu.make_async_copy(owner_hbm, owner_s, loc_sem.at[3]),
        pltpu.make_async_copy(node_hbm, node_s, loc_sem.at[4]),
        pltpu.make_async_copy(len_hbm, len_s, loc_sem.at[5]),
        pltpu.make_async_copy(
            q_hbm.at[:, pl.ds(pl.multiple_of(k * (GROUP * HD), HD), GROUP * HD)], q_all.at[x, k], loc_sem.at[6]
        ),
        pltpu.make_async_copy(nk_hbm.at[:, pl.ds(pl.multiple_of(k * HD, HD), HD)], nk.at[k], loc_sem.at[7]),
        pltpu.make_async_copy(nv_hbm.at[:, pl.ds(pl.multiple_of(k * HD, HD), HD)], nv.at[k], loc_sem.at[8]),
        pltpu.make_async_copy(sk_hbm, sk, loc_sem.at[9]),
        pltpu.make_async_copy(sv_hbm, sv, loc_sem.at[10]),
    ]
    for c in local:
        c.start()

    barrier = pltpu.get_barrier_semaphore()
    trees = [block_tree(half, j) for j in JUMPS]
    jumps = sorted({abs(e - d) for tree, _ in trees for e, d in tree.items()})
    peers = [at_z(s * d) for d in jumps for s in (1, -1)] + [at_x(d) for d in range(1, NX)] + [at_k(o) for o in range(1, nkv)]
    for dev in peers:
        pl.semaphore_signal(barrier, inc=1, device_id=dev, device_id_type=MESH)
    local[2].wait()
    flag = jnp.where(par_s[1] == 0, 0.0, LOW).astype(F32)
    k_all[z, 2 * BLK : 2 * BLK + FLAG] = jnp.full((FLAG, HD), flag, F32).astype(BF16)
    local[0].wait()
    local[1].wait()
    v_all[z] = v_nat[...].astype(F32).T.astype(BF16)
    pl.semaphore_wait(barrier, len(peers))

    done = [lag + max(stage.values()) + 1 for lag, (_, stage) in zip(LAGS, trees)]
    def chunk(ref, lo, hi):
        return lambda b: ref.at[b, lo:hi]

    chunks = [
        (0, chunk(k_all, 0, BLK), 0),
        (1, chunk(k_all, BLK, 2 * BLK + FLAG), 0),
        (2, chunk(v_all, 0, HD // 2), 1),
        (3, chunk(v_all, HD // 2, HD), 1),
    ]

    def carried(c, dirn, d):
        return d < half or c % 2 == dirn

    def hand_on(c, at, tree, d, dirn):
        sign = 1 - 2 * dirn
        block = (z - sign * d + nz) % nz
        for e in sorted((e for e in tree if tree[e] == d), reverse=True):
            if carried(c, dirn, e):
                ref = at(block)
                remote(ref, ref, ring_ss.at[dirn, c, e], ring_rs.at[dirn, c, e], at_z(sign * (e - d))).start()

    def arrive(c, at, d, dirn):
        sign = 1 - 2 * dirn
        if carried(c, dirn, d):
            ref = at((z - sign * d + nz) % nz)
            remote(ref, ref, ring_ss.at[dirn, c, d], ring_rs.at[dirn, c, d], at_z(sign)).wait_recv()

    def slot(t):
        for c, at, i in chunks:
            tree, stage = trees[i]
            for d in range(half + 1):
                if LAGS[i] + stage[d] != t:
                    continue
                for dirn in (0, 1):
                    if d > 0:
                        arrive(c, at, d, dirn)
                    hand_on(c, at, tree, d, dirn)

    def drain():
        for c, at, i in chunks:
            tree = trees[i][0]
            for d in range(1, half + 1):
                for dirn in (0, 1):
                    if carried(c, dirn, d):
                        ref = at((z - (1 - 2 * dirn) * tree[d] + nz) % nz)
                        remote(ref, ref, ring_ss.at[dirn, c, d], ring_rs.at[dirn, c, d], at_z(1)).wait_send()

    def a2a(i, o, got=False):
        to = (k + o) % nkv
        frm = (k + nkv - o) % nkv
        wide = pl.ds(pl.multiple_of(to * (GROUP * HD), HD), GROUP * HD)
        thin = pl.ds(pl.multiple_of(to * HD, HD), HD)
        src = (q_hbm.at[:, wide], nk_hbm.at[:, thin], nv_hbm.at[:, thin])[i]
        dst = (q_all.at[x], nk, nv)[i]
        if got:
            src, dst = dst.at[frm], dst.at[frm]
        else:
            dst = dst.at[k]
        return remote(src, dst, a2a_ss.at[i, o], a2a_rs.at[i, o], at_k(o))

    slot(0)
    for i in range(3):
        for o in range(1, nkv):
            a2a(i, o).start()

    local[3].wait()
    local[4].wait()
    local[5].wait()
    lane = lax.broadcasted_iota(I32, (1, HD), 1)
    own_z = own_x = nodes = jnp.zeros((1, HD), I32)
    for i in range(2 * nkv):
        own_z = jnp.where(lane == i, owner_s[i] % nz, own_z)
        own_x = jnp.where(lane == i, owner_s[i] // nz, own_x)
        nodes = jnp.where(lane == i, node_s[i], nodes)
    pad = jnp.zeros((5, HD), I32)
    meta[x] = jnp.concatenate([own_z, own_x, nodes, pad], axis=0)
    for d in range(1, NX):
        remote(meta.at[x], meta.at[x], m_ss.at[d], m_rs.at[d], at_x(d)).start()

    first = (lane // STEPS) % 2 == 0

    def both(a, b):
        return jnp.where(first, a, b)

    def pair_queries(src, p):
        slab = q_all[src, p]
        return jnp.concatenate([slab[:, j * HD : (j + 1) * HD] for j in range(GROUP)], axis=0)

    def send_queries():
        for o in range(1, nkv):
            a2a(0, o, True).wait_recv()
        local[6].wait()
        for d in (1, 3, 2):
            remote(q_all.at[x], q_all.at[x], x_ss.at[d], x_rs.at[d], at_x(d)).start()

    def await_queries(d):
        src = (x + d) % NX
        remote(q_all.at[src], q_all.at[src], x_ss.at[NX - d], x_rs.at[NX - d], at_x(d)).wait_recv()

    def await_meta():
        for d in range(1, NX):
            src = (x + d) % NX
            remote(meta.at[src], meta.at[src], m_ss.at[NX - d], m_rs.at[NX - d], at_x(d)).wait_recv()
        c = pltpu.make_async_copy(meta, meta_s, meta_sem.at[0])
        c.start()
        c.wait()

    def await_own():
        for o in range(1, nkv):
            a2a(1, o, True).wait_recv()
            a2a(2, o, True).wait_recv()
        for i in (7, 8, 9, 10):
            local[i].wait()

    def own_pair(i):
        p = pair(i)
        queries = pair_queries(x, p)
        len_a, len_b = len_s[2 * p], len_s[2 * p + 1]
        s_suf = both(dot(sk[2 * p], queries, NT), dot(sk[2 * p + 1], queries, NT))
        s_new = dot(nk[p], queries, NT)
        pos = lax.broadcasted_iota(I32, (SUF, HD), 0)
        s_suf = jnp.where(pos < both(len_a, len_b), s_suf, LOW)
        row = lax.broadcasted_iota(I32, (rows2, HD), 0)
        col = lax.broadcasted_iota(I32, (rows2, HD), 1)
        seen = (row // STEPS == (col // STEPS) % 2) & (row % STEPS <= col % STEPS)
        s_new = jnp.where(seen, s_new, LOW)
        peak = jnp.maximum(jnp.max(s_suf, axis=0, keepdims=True), jnp.max(s_new, axis=0, keepdims=True))
        w_suf = jnp.exp2((s_suf - peak) * EXPO)
        w_new = jnp.exp2((s_new - peak) * EXPO)
        total = jnp.sum(w_suf, axis=0, keepdims=True) + jnp.sum(w_new, axis=0, keepdims=True)
        w_suf, w_new = w_suf.astype(BF16), w_new.astype(BF16)
        va = sv[2 * p].astype(F32).T.astype(BF16)
        vb = sv[2 * p + 1].astype(F32).T.astype(BF16)
        vn = nv[p].astype(F32).T.astype(BF16)
        own_num[i] = both(dot(va, w_suf), dot(vb, w_suf)) + dot(vn, w_new)
        st_own[0, i : i + 1] = peak
        st_own[1, i : i + 1] = total

    def prompt_weights(d, i):
        src, p = (x + d) % NX, pair(i)
        a, b = 2 * p, 2 * p + 1
        queries = pair_queries(src, p)
        ka, kb = meta_s[src, 0, a], meta_s[src, 0, b]
        node_a, node_b = meta_s[src, 2, a], meta_s[src, 2, b]
        s = both(dot(k_all[ka, 0 : 2 * BLK], queries, NT), dot(k_all[kb, 0 : 2 * BLK], queries, NT))
        flag_a = k_all[ka, 2 * BLK : 2 * BLK + FLAG].astype(F32)[0:1]
        flag_b = k_all[kb, 2 * BLK : 2 * BLK + FLAG].astype(F32)[0:1]
        nodes_ab = both(node_a, node_b)
        s0 = s[0:BLK] + jnp.where(nodes_ab == 1, both(flag_a, flag_b), 0.0)
        s1 = s[BLK:] + jnp.where(nodes_ab == 1, 0.0, LOW)
        peak = jnp.max(jnp.maximum(s0, s1), axis=0, keepdims=True)
        w0 = jnp.exp2((s0 - peak) * EXPO)
        w1 = jnp.exp2((s1 - peak) * EXPO)
        st_p[d, 0, i : i + 1] = peak
        st_p[d, 1, i : i + 1] = jnp.sum(w0 + w1, axis=0, keepdims=True)
        w_all[d, i, 0:BLK] = w0.astype(BF16)
        w_all[d, i, BLK:] = w1.astype(BF16)

    def send_stats(d):
        e = NX - d
        remote(st_p.at[d], st_in.at[e], st_ss.at[d], st_rs.at[e], at_x(d)).start()

    def prompt_values(d, i):
        src, p = (x + d) % NX, pair(i)
        w = w_all[d, i]
        num = both(dot(v_all[meta_s[src, 0, 2 * p]], w), dot(v_all[meta_s[src, 0, 2 * p + 1]], w))
        ret[d, i] = num.astype(BF16)

    def owner_side(src, i):
        p = pair(i)
        return both((meta_s[src, 1, 2 * p] - x + NX) % NX, (meta_s[src, 1, 2 * p + 1] - x + NX) % NX)

    def places(high, s):
        lo = high * mid + s * sub
        return slice(lo, lo + sub)

    routes = [
        (lambda s: ret.at[2, places(0, s)], lambda s: relay.at[0, s * sub : (s + 1) * sub], -1),
        (lambda s: ret.at[2, places(1, s)], lambda s: relay.at[1, s * sub : (s + 1) * sub], 1),
        (lambda s: ret.at[3, places(1, s)], lambda s: ret_in.at[0, places(1, s)], -1),
        (lambda s: ret.at[1, places(0, s)], lambda s: ret_in.at[1, places(0, s)], 1),
        (lambda s: ret.at[3, places(0, s)], lambda s: ret_in.at[0, places(0, s)], -1),
        (lambda s: ret.at[1, places(1, s)], lambda s: ret_in.at[1, places(1, s)], 1),
    ]

    def back(n, s):
        src, dst, step = routes[n]
        return remote(src(s), dst(s), ret_ss.at[n, s], ret_rs.at[n, s], at_x(step + NX))

    def arrived(n, s):
        dst = routes[n][1](s)
        remote(dst, dst, ret_ss.at[n, s], ret_rs.at[n, s], at_x(1)).wait_recv()

    def put_between(high, s):
        d, far = (1, 3) if high else (3, 1)
        for i in range(nkv)[places(high, s)]:
            there = owner_side((x + d) % NX, i) == far
            ret[d, i] = jnp.where(there, relay[high, i - high * mid].astype(F32), ret[d, i].astype(F32)).astype(BF16)

    def factors():
        for e in range(1, NX):
            remote(st_in.at[e], st_in.at[e], st_ss.at[e], st_rs.at[e], at_x(e)).wait_recv()
        for i in range(nkv):
            side = owner_side(x, i)
            row = slice(i, i + 1)
            peak, total = st_p[0, 0, row], st_p[0, 1, row]
            for e in range(1, NX):
                peak = jnp.where(side == e, st_in[e, 0, row], peak)
                total = jnp.where(side == e, st_in[e, 1, row], total)
            peak_own, total_own = st_own[0, row], st_own[1, row]
            top = jnp.maximum(peak, peak_own)
            f_p = jnp.exp2((peak - top) * EXPO)
            f_o = jnp.exp2((peak_own - top) * EXPO)
            inv = 1.0 / (f_p * total + f_o * total_own)
            fac[0, row] = f_p * inv
            fac[1, row] = f_o * inv

    def merge(i):
        side = owner_side(x, i)
        right = (side == 1) | (side == 2) if i < mid else side == 1
        num = jnp.where(right, ret_in[0, i].astype(F32), ret_in[1, i].astype(F32))
        num = jnp.where(side == 0, ret[0, i].astype(F32), num)
        out = num * fac[0, i : i + 1] + own_num[i] * fac[1, i : i + 1]
        fin_out[i] = out.astype(BF16)
        if i < nkv - 1:
            remote(fin_out.at[i], fin.at[i], fin_ss.at[i], fin_rs.at[i], (r, pair(i))).start()

    def final(i):
        if i < nkv - 1:
            remote(fin.at[i], fin.at[i], fin_ss.at[i], fin_rs.at[i], at_k(1)).wait_recv()
            rows = fin[i]
        else:
            rows = fin_out[i]
        rows = rows.astype(F32).T.astype(BF16)
        g = (k + 2 * nkv - 1 - i) % nkv
        for j in range(GROUP):
            at = pl.ds(pl.multiple_of((g * GROUP + j) * HD, HD), HD)
            out_ref[:, at] = rows[j * rows2 : (j + 1) * rows2]

    last = max(done)
    before = {t: [] for t in range(1, last + 1)}

    def plan(t, f, *args):
        before[min(t, last)].append(functools.partial(f, *args))

    plan(2, send_queries)
    plan(3, await_own)
    for p in range(nkv):
        plan(3 + (p * 3) // nkv, own_pair, p)
    plan(min(6, done[0]), await_meta)

    def spread(work, start, end):
        for i, (d, p) in enumerate(work):
            t = start + (i * max(end - start, 1)) // len(work)
            yield t, d, p

    order = [(d, p) for d in (0, 1, 3, 2) for p in range(nkv)]
    for t, d, p in spread(order, done[0], done[1]):
        if p == 0 and d:
            plan(t, await_queries, d)
        plan(t, prompt_weights, d, p)
        if p == nkv - 1 and d:
            plan(t, send_stats, d)
    for t in range(1, last + 1):
        for f in before[t]:
            f()
        if t < last:
            slot(t)

    ways = [(high, s) for s in range(parts) for high in (0, 1)]
    for high, s in ways:
        for i in range(nkv)[places(high, s)]:
            prompt_values(2, i)
        back(high, s).start()
    for high, s in ways:
        d = 3 if high else 1
        for i in range(nkv)[places(high, s)]:
            prompt_values(d, i)
        back(2 if high else 3, s).start()
    for high, s in ways:
        d = 1 if high else 3
        for i in range(nkv)[places(high, s)]:
            prompt_values(d, i)
    for i in range(nkv):
        prompt_values(0, i)
    for high, s in ways:
        arrived(high, s)
        put_between(high, s)
        back(4 + high, s).start()
    factors()
    for high, s in ways:
        arrived(2 if high else 3, s)
    for high, s in ways:
        arrived(4 + high, s)
        for i in range(nkv)[places(high, s)]:
            merge(i)
    final(nkv - 1)
    for high, s in ways:
        for i in range(nkv)[places(high, s)]:
            if i < nkv - 1:
                final(i)

    drain()
    for o in range(1, nkv):
        for i in range(3):
            a2a(i, o).wait_send()
    for i in range(nkv - 1):
        remote(fin_out.at[i], fin.at[i], fin_ss.at[i], fin_rs.at[i], at_k(1)).wait_send()
    for d in range(1, NX):
        remote(q_all.at[x], q_all.at[x], x_ss.at[d], x_rs.at[d], at_x(d)).wait_send()
        remote(meta.at[x], meta.at[x], m_ss.at[d], m_rs.at[d], at_x(d)).wait_send()
        remote(st_p.at[d], st_in.at[d], st_ss.at[d], st_rs.at[d], at_x(d)).wait_send()
    for n in range(len(routes)):
        for s in range(parts):
            back(n, s).wait_send()


def solution(mesh):
    nz = mesh.shape["req"] // NX
    nkv = mesh.shape["kv"]
    half = nz // 2
    mid = nkv // 2
    parts = mid // max(mid // 4, 1)
    rows2 = 2 * STEPS

    def shards(q, nk, nv, sk, sv, length, pk, pv, parent, owner, node):
        q = q.reshape(rows2, -1)
        nk = nk.reshape(rows2, -1)
        nv = nv.reshape(rows2, -1)
        pk = pk.reshape(2 * BLK, HD)
        pv = pv.reshape(2 * BLK, HD)
        dma = pltpu.SemaphoreType.DMA
        q, nk, nv, sk, sv, pk, pv, length, parent, owner, node = (
            pltpu.with_memory_space_constraint(a, pltpu.HBM)
            for a in (q, nk, nv, sk, sv, pk, pv, length, parent, owner, node)
        )
        vmem = pltpu.VMEM
        out = pl.pallas_call(
            functools.partial(kernel, nz, nkv),
            out_shape=jax.ShapeDtypeStruct((rows2, nkv * GROUP * HD), BF16),
            in_specs=[pl.BlockSpec(memory_space=pltpu.HBM)] * 11,
            out_specs=pl.BlockSpec(memory_space=pltpu.VMEM),
            scratch_shapes=[
                vmem((nz, 2 * BLK + FLAG, HD), BF16),
                vmem((2 * BLK, HD), BF16),
                vmem((nz, HD, 2 * BLK), BF16),
                vmem((NX, nkv, rows2, GROUP * HD), BF16),
                vmem((nkv, rows2, HD), BF16),
                vmem((nkv, rows2, HD), BF16),
                vmem((2 * nkv, SUF, HD), BF16),
                vmem((2 * nkv, SUF, HD), BF16),
                vmem((NX, 8, HD), I32),
                pltpu.SMEM((NX, 8, HD), I32),
                pltpu.SMEM((2 * nkv,), I32),
                pltpu.SMEM((2,), I32),
                pltpu.SMEM((2 * nkv,), I32),
                pltpu.SMEM((2 * nkv,), I32),
                vmem((NX, nkv, 2 * BLK, HD), BF16),
                vmem((NX, 2, nkv, HD), F32),
                vmem((NX, 2, nkv, HD), F32),
                vmem((2, nkv, HD), F32),
                vmem((nkv, HD, HD), F32),
                vmem((2, nkv, HD), F32),
                vmem((NX, nkv, HD, HD), BF16),
                vmem((2, mid, HD, HD), BF16),
                vmem((2, nkv, HD, HD), BF16),
                vmem((nkv, HD, HD), BF16),
                vmem((nkv, HD, HD), BF16),
                dma((11,)),
                dma((1,)),
                dma((2, 4, half + 1)),
                dma((2, 4, half + 1)),
                dma((3, nkv)),
                dma((3, nkv)),
                dma((NX,)),
                dma((NX,)),
                dma((NX,)),
                dma((NX,)),
                dma((NX,)),
                dma((NX,)),
                dma((6, parts)),
                dma((6, parts)),
                dma((nkv,)),
                dma((nkv,)),
            ],
            compiler_params=pltpu.CompilerParams(
                collective_id=0, has_side_effects=True, vmem_limit_bytes=32 * 2**20
            ),
        )(q, nk, nv, sk, sv, pk, pv, length, parent, owner, node)
        return out.reshape(2, STEPS, -1)

    in_specs = (
        P(("req", "kv"), None, None),
        P(("req", "kv"), None, None),
        P(("req", "kv"), None, None),
        P("req", None, "kv"),
        P("req", None, "kv"),
        P("req"),
        P("req", None, "kv"),
        P("req", None, "kv"),
        P("req"),
        P("req"),
        P("req"),
    )
    return jax.shard_map(
        shards, mesh=mesh, in_specs=in_specs, out_specs=P(("req", "kv"), None, None), check_vma=False
    )
```
